32 devices in a mesh: grp: 2 (over y), panel: 4 (over z), tok: 2 (over x), rep: 2 (over core).
Axes of the slice: x: 2, y: 2, z: 4, core: 2. Of those that a mesh axis runs over, the one named last changes fastest.
Arguments:
- grads: bfloat16 [8, 512, 32768], P(('grp', 'rep'), 'tok', 'panel'), parts along dimension 0, may hold values from -6 to 6
- acts: bfloat16 [8, 512, 8192], P(('grp', 'rep'), 'tok', 'panel'), parts along dimension 0, may hold values from -6 to 6
- out_basis: bfloat16 [32768, 256], P('panel', ('tok', 'rep')), may hold values from -0.03125 to 0.03125
- in_basis: bfloat16 [8192, 128], P('panel'), may hold values from -0.0625 to 0.0625
- eigvals: float32 [256, 128], P('panel'), may hold values from 0.05 to 5
- query_rot: bfloat16 [128, 256, 128], P('grp', 'panel'), parts along dimension 0, may hold values from -0.0014648438 to 0.0014648438
- lengths: int32 [8], P(('grp', 'rep')), parts along dimension 0, may hold values from 128 to 512
- token_mask: int32 [8, 512], P(('grp', 'rep'), 'tok'), parts along dimension 0, may hold values 0 or 1
- failure_ids: int32 [128], P('grp'), parts along dimension 0, may hold values from 0 to 7, as said below
Outputs:
- query_scores: float32 [64, 8], P(None, ('grp', 'rep')), parts along dimension 1
- influence: float32 [8, 8], P(None, ('grp', 'rep')), parts along dimension 1
The draws below stay inside these ranges and needn't reach their ends.
There are 2 independent parts, one for each index of `grp`. The reference program is written for one: setup_inputs(seed, part) draws one part's arguments, and reference() takes and returns one part's arrays. A program takes and returns all parts, laid end to end along the dimension named above; an argument that names none is the same for every part. Nothing has to cross between parts.
Inputs may be any that keep to these rules, and one draw needn't show every extreme that they name: `failure_ids`: at least one failure other than 0 and 7 has no query.
All inputs are finite; a program needn't handle non-finite values. No bound on the sum of `token_mask` on one device may be relied on, other than what follows from the above.
Results may differ from the reference program's by a relative error of at most 0.0049.
Values may be sent and summed in bfloat16 or wider, within the bound.
A program may use at most 64 MiB of HBM per device.

```python
import math
import jax
import jax.numpy as jnp
from jax import lax

D = 8192
FF = 32768
KA = 128
QUERIES = 64
NFAIL = 8
KS = 256
SEQS = 4
LEN = 512


def draw_failure_ids(key, part):
    key = jax.random.fold_in(key, 11)
    key_list = jax.random.split(key, 4)
    empty_fail = jax.random.randint(key_list[0], (), 1, NFAIL - 1)
    drawn_ids = jax.random.randint(key_list[1], (QUERIES,), 0, NFAIL - 1)
    first_slot = jax.random.randint(key_list[2], (), 0, QUERIES)
    second_slot = (first_slot + jax.random.randint(key_list[3], (), 1, QUERIES)) % QUERIES
    positions = jnp.arange(QUERIES, dtype=jnp.int32)
    drawn_ids = jnp.where(positions == first_slot, 0, drawn_ids)
    drawn_ids = jnp.where(positions == second_slot, NFAIL - 2, drawn_ids)
    return (drawn_ids + (drawn_ids >= empty_fail).astype(jnp.int32)).astype(jnp.int32)


def with_ends(drawn, key, low, top_value):
    longest = drawn.shape.index(max(drawn.shape))
    spots = []
    for shift in (0, 1):
        where = [jax.random.randint(jax.random.fold_in(key, axis), (), 0, length) for axis, length in enumerate(drawn.shape)]
        where[longest] = (where[longest] + shift) % drawn.shape[longest]
        spots.append(tuple(where))
    return drawn.at[spots[0]].set(low).at[spots[1]].set(top_value)


def shard_levels(own_key, shape, pieces, smallest, top_value):
    def one(dim, shards_of):
        draws = jax.random.uniform(jax.random.fold_in(jax.random.fold_in(own_key, 6), dim), (shards_of,), jnp.float32, smallest / len(pieces), top_value / len(pieces))
        return jnp.repeat(jnp.exp(draws), shape[dim] // shards_of).reshape((-1,) + (1,) * (len(shape) - dim - 1))

    gain = one(*pieces[0])
    for cut in pieces[1:]:
        gain = gain * one(*cut)
    return gain


def noise(rng, extent, width, bound, cuts=(), kind=jnp.bfloat16):
    entries = jax.random.normal(rng, extent, jnp.float32) * width
    if len(cuts) > 0:
        entries = shard_levels(rng, extent, cuts, -0.22, 0.18) * entries
    return jnp.clip(entries, min=-bound, max=bound).astype(kind)


def setup_inputs(seed: int = 0, part: int = 0) -> dict:
    key_of = jax.random.split(jax.random.key(seed), 10)
    own_keys = jax.random.split(jax.random.fold_in(key_of[9], part), 10)
    grads = noise(own_keys[0], (SEQS, LEN, FF), 1.0, 6.0, ((0, 2), (1, 2), (2, 4)))
    acts = noise(own_keys[1], (SEQS, LEN, D), 1.0, 6.0, ((0, 2), (1, 2), (2, 4)))
    out_basis = noise(key_of[2], (FF, KS), FF ** -0.5, 0.03125, ((0, 4), (1, 4)))
    in_basis = noise(key_of[3], (D, KA), D ** -0.5, 0.0625, ((0, 4),))
    eigvals = jnp.clip(jnp.exp(math.log(5.0) - 4.6051702 * jax.random.uniform(key_of[4], (KS, KA), jnp.float32) ** shard_levels(key_of[4], (KS, KA), ((0, 4),), -0.2, 0.2)), 0.05, 5.0)
    query_rot = noise(own_keys[5], (QUERIES, KS, KA), (KS * KA * LEN) ** -0.5, 0.0014648438, ((1, 4),))
    lengths = with_ends(jax.random.randint(own_keys[6], (SEQS,), LEN // 4, LEN + 1), jax.random.fold_in(own_keys[6], 1), LEN // 4, LEN).astype(jnp.int32)
    token_mask = with_ends((jax.random.randint(own_keys[7], (SEQS, LEN), 0, 8) < 7).astype(jnp.int32), jax.random.fold_in(own_keys[7], 1), 0, 1)
    failure_ids = draw_failure_ids(jax.random.fold_in(jax.random.fold_in(key_of[9], part), 71), part)
    return dict(grads=grads, acts=acts, out_basis=out_basis, in_basis=in_basis, eigvals=eigvals, query_rot=query_rot, lengths=lengths, token_mask=token_mask, failure_ids=failure_ids)


damping = 0.1


def reference(grads, acts, out_basis, in_basis, eigvals, query_rot, lengths, token_mask, failure_ids):
    rows = SEQS * LEN
    proj_out = jnp.dot(grads.reshape(rows, FF), out_basis, preferred_element_type=jnp.float32)
    proj_in = jnp.dot(acts.reshape(rows, D), in_basis, preferred_element_type=jnp.float32).astype(jnp.bfloat16)
    weighted = (query_rot.astype(jnp.float32) / (eigvals + damping)).astype(jnp.bfloat16)
    positions = jnp.arange(LEN, dtype=jnp.int32)
    valid = ((positions[None, :] < lengths[:, None]) & (token_mask == 1)).astype(jnp.float32).reshape(rows)

    def one_query(weight_one):
        mixed = jnp.dot(proj_in, weight_one.T, preferred_element_type=jnp.float32)
        token_score = jnp.sum(mixed * proj_out, axis=1)
        return jnp.sum((token_score * valid).reshape(SEQS, LEN), axis=1)

    query_scores = lax.map(one_query, weighted)
    onehot = (failure_ids[None, :] == jnp.arange(NFAIL, dtype=jnp.int32)[:, None]).astype(jnp.float32)
    counts = jnp.maximum(jnp.sum(onehot, axis=1), 1.0)
    influence = jnp.dot(onehot, query_scores, precision=lax.Precision.HIGHEST) / counts[:, None]
    return query_scores, influence
```

```python
import functools

import jax
import jax.numpy as jnp
from jax import lax
from jax.experimental import pallas as pl
from jax.experimental.pallas import tpu as pltpu
from jax.sharding import PartitionSpec as P

NFAIL = 8
DAMPING = 0.1
MESH = pl.DeviceIdType.MESH
F32 = jnp.float32
BF16 = jnp.bfloat16
NT = (((1,), (1,)), ((), ()))
TN = (((0,), (0,)), ((), ()))


def each(count, body):
    if count <= 8:
        for index in range(count):
            body(index)
    else:
        pl.loop(0, count)(body)


def kernel(
    sizes,
    grads_hbm, acts_hbm, basis_hbm, inb_hbm, eig_ref, qrot_hbm, len_ref, mask_ref, fail_ref,
    score_ref, infl_ref,
    grads, acts, inb, basis, qrot, weight, proj, in_send, in_recv, pin, pinv,
    m_send, m_recv, m_sum, s_send, s_recv,
    load_sem, grad_sem, own_send, own_recv, x_send, x_recv, y_send, y_recv,
    cx_send, cx_recv, cy_send, cy_recv,
    a_send, a_recv, g_send, g_recv, ms_sem, mr_sem, ss_sem, sr_sem,
):
    np_, nt, nc, ngrad = sizes
    grp, panel = lax.axis_index("grp"), lax.axis_index("panel")
    tok, rep = lax.axis_index("tok"), lax.axis_index("rep")
    seqs, length, hidden = grads.shape
    rows = seqs * length
    queries, kb, ka = qrot.shape
    cols = basis_hbm.shape[0]
    pair = 2 * cols
    npc = pair // kb
    half = hidden // 2
    cw = half // nc
    prow = rows // np_
    gstep = hidden // ngrad

    loads = [
        pltpu.make_async_copy(acts_hbm, acts, load_sem.at[0]),
        pltpu.make_async_copy(inb_hbm, inb, load_sem.at[1]),
        pltpu.make_async_copy(qrot_hbm, qrot, load_sem.at[2]),
    ]
    own_rows = pl.ds(pl.multiple_of((tok * 2 + rep) * cols, cols), cols)
    own_load = pltpu.make_async_copy(basis_hbm, basis.at[own_rows], load_sem.at[3])
    loads[0].start()
    loads[1].start()

    barrier = pltpu.get_barrier_semaphore()
    pl.semaphore_signal(barrier, inc=1, device_id={"rep": 1 - rep}, device_id_type=MESH)
    pl.semaphore_signal(barrier, inc=1, device_id={"grp": 1 - grp}, device_id_type=MESH)

    def other(index):
        shift = index + 1
        dp, dt = shift // nt, shift % nt
        return lax.rem(panel + dp, np_), lax.rem(tok + dt, nt)

    def greet(index):
        p, t = other(index)
        pl.semaphore_signal(barrier, inc=1, device_id={"panel": p, "tok": t}, device_id_type=MESH)

    each(np_ * nt - 1, greet)
    own_load.start()
    grad_loads = []
    for g in range(ngrad):
        at = pl.ds(g * gstep, gstep)
        grad_loads.append(
            pltpu.make_async_copy(grads_hbm.at[:, :, at], grads.at[:, :, at], grad_sem.at[g])
        )
    for copy in grad_loads:
        copy.start()
    loads[2].start()
    pl.semaphore_wait(barrier, np_ * nt + 1)

    def lanes(part, i):
        return pl.ds(pl.multiple_of(part * half + i * cw, cw), cw)

    def block(t, r):
        return pl.ds(pl.multiple_of((t * 2 + r) * cols, cols), cols)

    def remote(src, dst, send, recv, where):
        return pltpu.make_async_remote_copy(
            src_ref=src, dst_ref=dst, send_sem=send, recv_sem=recv,
            device_id=where, device_id_type=MESH,
        )

    def x_copy(d, i):
        at = lanes(grp, i)
        return remote(
            basis_hbm.at[:, at], basis.at[own_rows, at], x_send.at[d, i], x_recv.at[d, i],
            {"tok": lax.rem(tok + d + 1, nt)},
        )

    def from_tok(d):
        return lax.rem(tok + nt - d - 1, nt)

    def pass_copy(d, i, part, r, send, recv, where):
        at = basis.at[block(from_tok(d), r), lanes(part, i)]
        return remote(at, at, send.at[d, i], recv.at[d, i], where)

    def y_copy(d, i, part):
        return pass_copy(d, i, part, rep, y_send, y_recv, {"grp": 1 - grp})

    def cx_copy(d, i, r):
        return pass_copy(d, i, grp, r, cx_send, cx_recv, {"rep": 1 - rep})

    def cy_copy(d, i, r):
        return pass_copy(d, i, 1 - grp, r, cy_send, cy_recv, {"rep": 1 - rep})

    own_copy = remote(basis_hbm, basis.at[own_rows], own_send, own_recv, {"rep": 1 - rep})
    for i in range(nc):
        for d in range(nt - 1):
            x_copy(d, i).start()
        if i == 0:
            own_copy.start()

    loads[0].wait()
    loads[1].wait()
    in_part = jnp.dot(
        acts[...].reshape(rows, acts.shape[2]), inb[...], preferred_element_type=F32
    )
    in_send[...] = in_part.astype(BF16)

    def rows_of(p):
        return pl.ds(pl.multiple_of(p * prow, prow), prow)

    def a_copy(p):
        return remote(
            in_send.at[rows_of(p)], in_recv.at[panel], a_send.at[p], a_recv.at[panel],
            {"panel": p},
        )

    def a_from(p):
        return remote(
            in_send.at[rows_of(p)], in_recv.at[p], a_send.at[p], a_recv.at[p], {"panel": p}
        )

    def g_copy(p):
        mine = pin.at[rows_of(panel)]
        return remote(mine, mine, g_send.at[p], g_recv.at[panel], {"panel": p})

    def g_from(p):
        theirs = pin.at[rows_of(p)]
        return remote(theirs, theirs, g_send.at[p], g_recv.at[p], {"panel": p})

    def panels(body):
        each(np_ - 1, lambda index: body(lax.rem(panel + index + 1, np_)))

    panels(lambda p: a_copy(p).start())

    def sum_in():
        panels(lambda p: a_from(p).wait_recv())
        in_recv[panel] = in_send[rows_of(panel), :]
        total = in_recv[0].astype(F32)
        for p in range(1, np_):
            total = total + in_recv[p].astype(F32)
        pin[rows_of(panel), :] = total.astype(BF16)
        panels(lambda p: g_copy(p).start())

    def weigh():
        loads[2].wait()
        inverse = 1.0 / (eig_ref[...] + DAMPING)
        for q in range(0, queries, 8):
            w = qrot[q : q + 8].astype(F32) * inverse[None]
            w = w.astype(BF16).astype(F32)
            weight[:, q : q + 8, :] = jnp.swapaxes(w, 0, 1)
        s_send[...] = jnp.zeros_like(s_send)
        for copy in grad_loads:
            copy.wait()

    def valid_in():
        panels(lambda p: g_from(p).wait_recv())
        spots = lax.broadcasted_iota(jnp.int32, (1, length), 1) + tok * length
        for s in range(seqs):
            keep = jnp.where((spots < len_ref[s]) & (mask_ref[s : s + 1, :] == 1), 1.0, 0.0)
            keep = jnp.broadcast_to(keep, (ka, length)).T.astype(BF16)
            at = pl.ds(s * length, length)
            pinv[at, :] = pin[at, :] * keep

    def add_proj(d, part_rows, at, first):
        value = lax.dot_general(
            grads[:, :, at].reshape(rows, at.size), basis[part_rows, at], NT,
            preferred_element_type=F32,
        )
        if first:
            proj[d] = value
        else:
            proj[d] += value

    def pair_rows(t):
        return pl.ds(pl.multiple_of(t * pair, pair), pair)

    def m_copy(p):
        return remote(
            m_send.at[p], m_recv.at[panel], ms_sem.at[p], mr_sem.at[panel], {"panel": p}
        )

    def m_from(p):
        return remote(m_send.at[p], m_recv.at[p], ms_sem.at[p], mr_sem.at[p], {"panel": p})

    def mix(d, t):
        for s in range(seqs):
            at = pl.ds(s * length, length)
            m = lax.dot_general(
                proj[d, at, :].astype(BF16), pinv[at, :], TN, preferred_element_type=F32
            )
            m_send[pl.ds(t * npc, npc), s] = m.astype(BF16).reshape(npc, kb, ka)
        for j in range(npc):
            p = t * npc + j

            @pl.when(p != panel)
            def _():
                m_copy(p).start()

            @pl.when(p == panel)
            def _():
                m_recv[p] = m_send[p]

    def own_proj():
        own_load.wait()
        own_copy.wait_recv()
        for g in range(ngrad):
            add_proj(0, pair_rows(tok), pl.ds(g * gstep, gstep), g == 0)

    def own_mix():
        valid_in()
        mix(0, tok)

    tasks = {0: [weigh], min(1, nc - 1): [sum_in], min(2, nc - 1): [own_proj]}
    tasks.setdefault(min(4, nc - 1), []).append(own_mix)
    for i in range(nc):
        for d in range(nt - 1):
            x_arrive = remote(
                basis_hbm.at[:, lanes(grp, i)], basis.at[block(from_tok(d), rep), lanes(grp, i)],
                x_send.at[d, i], x_recv.at[d, i], {"tok": from_tok(d)},
            )
            x_arrive.wait_recv()
            y_copy(d, i, grp).start()
            cx_copy(d, i, rep).start()
        for task in tasks.get(i, ()):
            task()
        for d in range(nt - 1):
            y_copy(d, i, 1 - grp).wait_recv()
            cy_copy(d, i, rep).start()
        for d in range(nt - 1):
            t = from_tok(d)
            cx_copy(d, i, 1 - rep).wait_recv()
            add_proj(d + 1, pair_rows(t), lanes(grp, i), i == 0)
            cy_copy(d, i, 1 - rep).wait_recv()
            add_proj(d + 1, pair_rows(t), lanes(1 - grp, i), False)
    for d in range(nt - 1):
        mix(d + 1, from_tok(d))

    panels(lambda p: m_from(p).wait_recv())
    total = m_recv[0].astype(F32)
    for p in range(1, np_):
        total = total + m_recv[p].astype(F32)
    m_sum[...] = total

    def step(k8, sums):
        sums = list(sums)
        for j in range(8):
            k = k8 * 8 + j
            w = weight[k]
            for s in range(seqs):
                sums[s] = sums[s] + w * m_sum[s, pl.ds(k, 1), :]
        return tuple(sums)

    sums = lax.fori_loop(
        0, kb // 8, step, tuple(jnp.zeros((queries, ka), F32) for _ in range(seqs))
    )
    ones = jnp.ones((8, ka), F32)
    for s in range(seqs):
        line = lax.dot_general(
            ones, sums[s], NT, precision=lax.Precision.HIGHEST, preferred_element_type=F32
        )
        s_send[s : s + 1, 0:queries] = line[0:1, :]

    me = panel * nt + tok

    def s_copy(index):
        p, t = other(index)
        return remote(
            s_send, s_recv.at[me], ss_sem.at[index], sr_sem.at[me], {"panel": p, "tok": t}
        )

    def s_from(index):
        p, t = other(index)
        who = p * nt + t
        return remote(
            s_send, s_recv.at[who], ss_sem.at[index], sr_sem.at[who], {"panel": p, "tok": t}
        )

    each(np_ * nt - 1, lambda index: s_copy(index).start())
    s_recv[me] = s_send[...]
    each(np_ * nt - 1, lambda index: s_from(index).wait_recv())
    scores = s_recv[0]
    for who in range(1, np_ * nt):
        scores = scores + s_recv[who]
    scores = scores[:, 0:queries]
    score_ref[...] = scores[0:seqs, :]
    hot = jnp.where(
        lax.broadcasted_iota(jnp.int32, (NFAIL, queries), 0) == fail_ref[...], 1.0, 0.0
    )
    sums_f = lax.dot_general(
        scores, hot, NT, precision=lax.Precision.HIGHEST, preferred_element_type=F32
    )
    counts = lax.dot_general(
        jnp.ones((8, queries), F32), hot, NT, precision=lax.Precision.HIGHEST,
        preferred_element_type=F32,
    )
    infl_ref[...] = (sums_f / jnp.maximum(counts, 1.0))[0:seqs, :]

    own_copy.wait_send()
    for i in range(nc):
        for d in range(nt - 1):
            x_copy(d, i).wait_send()
            y_copy(d, i, grp).wait_send()
            cx_copy(d, i, rep).wait_send()
            cy_copy(d, i, rep).wait_send()
    panels(lambda p: a_copy(p).wait_send())
    panels(lambda p: g_copy(p).wait_send())
    panels(lambda p: m_copy(p).wait_send())
    each(np_ * nt - 1, lambda index: s_copy(index).wait_send())


def per_device(
    np_, nt, grads, acts, out_basis, in_basis, eigvals, query_rot, lengths, token_mask, failure_ids
):
    seqs, length, hidden = grads.shape
    rows = seqs * length
    queries, kb, ka = query_rot.shape
    cols = out_basis.shape[1]
    nc = min(8, hidden // 256)
    ngrad = min(8, hidden // 256)
    dma = pltpu.SemaphoreType.DMA
    hop = (nt - 1, nc)
    scratch = [
        pltpu.VMEM(grads.shape, BF16),
        pltpu.VMEM(acts.shape, BF16),
        pltpu.VMEM(in_basis.shape, BF16),
        pltpu.VMEM((cols * nt * 2, hidden), BF16),
        pltpu.VMEM(query_rot.shape, BF16),
        pltpu.VMEM((kb, queries, ka), F32),
        pltpu.VMEM((nt, rows, 2 * cols), F32),
        pltpu.VMEM((rows, ka), BF16),
        pltpu.VMEM((np_, rows // np_, ka), BF16),
        pltpu.VMEM((rows, ka), BF16),
        pltpu.VMEM((rows, ka), BF16),
        pltpu.VMEM((np_, seqs, kb, ka), BF16),
        pltpu.VMEM((np_, seqs, kb, ka), BF16),
        pltpu.VMEM((seqs, kb, ka), F32),
        pltpu.VMEM((8, 128), F32),
        pltpu.VMEM((np_ * nt, 8, 128), F32),
        dma((4,)),
        dma((ngrad,)),
        dma, dma,
        dma(hop), dma(hop), dma(hop), dma(hop),
        dma(hop), dma(hop), dma(hop), dma(hop),
        dma((np_,)), dma((np_,)), dma((np_,)), dma((np_,)),
        dma((np_,)), dma((np_,)),
        dma((np_ * nt,)), dma((np_ * nt,)),
    ]
    hbm = pl.BlockSpec(memory_space=pl.ANY)
    vmem = pl.BlockSpec(memory_space=pltpu.VMEM)
    scores, influence = pl.pallas_call(
        functools.partial(kernel, (np_, nt, nc, ngrad)),
        out_shape=(
            jax.ShapeDtypeStruct((seqs, queries), F32),
            jax.ShapeDtypeStruct((seqs, NFAIL), F32),
        ),
        in_specs=[
            hbm, hbm, hbm, hbm, vmem, hbm, pl.BlockSpec(memory_space=pltpu.SMEM), vmem, vmem
        ],
        out_specs=(vmem, vmem),
        scratch_shapes=scratch,
        compiler_params=pltpu.CompilerParams(
            collective_id=0, has_side_effects=True, vmem_limit_bytes=56 * 1024 * 1024
        ),
        name="influence",
    )(
        grads, acts, out_basis.T, in_basis, eigvals, query_rot, lengths, token_mask,
        failure_ids[None, :],
    )
    return scores.T, influence.T


def solution(mesh):
    in_specs = (
        P(("grp", "rep"), "tok", "panel"),
        P(("grp", "rep"), "tok", "panel"),
        P("panel", ("tok", "rep")),
        P("panel", None),
        P("panel", None),
        P("grp", "panel", None),
        P(("grp", "rep")),
        P(("grp", "rep"), "tok"),
        P("grp"),
    )
    out_specs = (P(None, ("grp", "rep")), P(None, ("grp", "rep")))
    return jax.shard_map(
        functools.partial(per_device, mesh.shape["panel"], mesh.shape["tok"]),
        mesh=mesh, in_specs=in_specs, out_specs=out_specs, check_vma=False,
    )
```

```python
import functools

import jax
import jax.numpy as jnp
from jax import lax
from jax.experimental import pallas as pl
from jax.experimental.pallas import tpu as pltpu
from jax.sharding import PartitionSpec as P

NFAIL = 8
DAMPING = 0.1
MESH = pl.DeviceIdType.MESH
F32 = jnp.float32
BF16 = jnp.bfloat16
NT = (((1,), (1,)), ((), ()))
TN = (((0,), (0,)), ((), ()))


def each(count, body):
    if count <= 8:
        for index in range(count):
            body(index)
    else:
        pl.loop(0, count)(body)


def kernel(
    sizes,
    grads_hbm, acts_hbm, basis_hbm, inb_hbm, eig_ref, qrot_hbm, len_ref, mask_ref,
    total_ref,
    grads, acts, inb, basis, qrot, weight, proj, in_send, in_recv, pin, pinv,
    m_send, m_recv, m_sum, s_send, s_recv,
    load_sem, grad_sem, own_sem, own_send, own_recv, x_send, x_recv, y_send, y_recv,
    cx_send, cx_recv, cy_send, cy_recv,
    a_send, a_recv, g_send, g_recv, ms_sem, mr_sem, ss_sem, sr_sem,
):
    np_, nt, nc, ngrad = sizes
    grp, panel = lax.axis_index("grp"), lax.axis_index("panel")
    tok, rep = lax.axis_index("tok"), lax.axis_index("rep")
    seqs, length, hidden = grads.shape
    rows = seqs * length
    queries, kb, ka = qrot.shape
    cols = basis_hbm.shape[0]
    pair = 2 * cols
    npc = pair // kb
    half = hidden // 2
    cw = half // nc
    prow = rows // np_
    gstep = hidden // ngrad

    loads = [
        pltpu.make_async_copy(acts_hbm, acts, load_sem.at[0]),
        pltpu.make_async_copy(inb_hbm, inb, load_sem.at[1]),
        pltpu.make_async_copy(qrot_hbm, qrot, load_sem.at[2]),
    ]
    own_rows = pl.ds(pl.multiple_of((tok * 2 + rep) * cols, cols), cols)
    own_loads = []
    for j in range(2 * nc):
        own_loads.append(
            pltpu.make_async_copy(
                basis_hbm.at[:, pl.ds(j * cw, cw)], basis.at[j, own_rows], own_sem.at[j]
            )
        )
    for copy in own_loads:
        copy.start()
    loads[0].start()
    loads[1].start()

    barrier = pltpu.get_barrier_semaphore()
    pl.semaphore_signal(barrier, inc=1, device_id={"rep": 1 - rep}, device_id_type=MESH)
    pl.semaphore_signal(barrier, inc=1, device_id={"grp": 1 - grp}, device_id_type=MESH)

    def other(index):
        shift = index + 1
        dp, dt = shift // nt, shift % nt
        return lax.rem(panel + dp, np_), lax.rem(tok + dt, nt)

    def greet(index):
        p, t = other(index)
        pl.semaphore_signal(barrier, inc=1, device_id={"panel": p, "tok": t}, device_id_type=MESH)

    each(np_ * nt - 1, greet)
    grad_loads = []
    for g in range(ngrad):
        at = pl.ds(g * gstep, gstep)
        grad_loads.append(
            pltpu.make_async_copy(grads_hbm.at[:, :, at], grads.at[:, :, at], grad_sem.at[g])
        )
    for copy in grad_loads:
        copy.start()
    loads[2].start()
    pl.semaphore_wait(barrier, np_ * nt + 1)

    def block(t, r):
        return pl.ds(pl.multiple_of((t * 2 + r) * cols, cols), cols)

    def remote(src, dst, send, recv, where):
        return pltpu.make_async_remote_copy(
            src_ref=src, dst_ref=dst, send_sem=send, recv_sem=recv,
            device_id=where, device_id_type=MESH,
        )

    def x_copy(d, i):
        mine = basis.at[grp * nc + i, own_rows]
        return remote(
            mine, mine, x_send.at[d, i], x_recv.at[d, i],
            {"tok": lax.rem(tok + d + 1, nt)},
        )

    def from_tok(d):
        return lax.rem(tok + nt - d - 1, nt)

    def pass_copy(d, i, part, r, send, recv, where):
        at = basis.at[part * nc + i, block(from_tok(d), r)]
        return remote(at, at, send.at[d, i], recv.at[d, i], where)

    def y_copy(d, i, part):
        return pass_copy(d, i, part, rep, y_send, y_recv, {"grp": 1 - grp})

    def cx_copy(d, i, r):
        return pass_copy(d, i, grp, r, cx_send, cx_recv, {"rep": 1 - rep})

    def cy_copy(d, i, r):
        return pass_copy(d, i, 1 - grp, r, cy_send, cy_recv, {"rep": 1 - rep})

    own_copy = remote(basis.at[:, own_rows], basis.at[:, own_rows], own_send, own_recv, {"rep": 1 - rep})
    for copy in own_loads:
        copy.wait()

    @pl.loop(0, nc)
    def _(i):
        for d in range(nt - 1):
            x_copy(d, i).start()

    own_copy.start()

    loads[0].wait()
    loads[1].wait()
    in_part = jnp.dot(
        acts[...].reshape(rows, acts.shape[2]), inb[...], preferred_element_type=F32
    )
    in_send[...] = in_part

    def rows_of(p):
        return pl.ds(pl.multiple_of(p * prow, prow), prow)

    def a_copy(p):
        return remote(
            in_send.at[rows_of(p)], in_recv.at[panel], a_send.at[p], a_recv.at[panel],
            {"panel": p},
        )

    def a_from(p):
        return remote(
            in_send.at[rows_of(p)], in_recv.at[p], a_send.at[p], a_recv.at[p], {"panel": p}
        )

    def g_copy(p):
        mine = pin.at[rows_of(panel)]
        return remote(mine, mine, g_send.at[p], g_recv.at[panel], {"panel": p})

    def g_from(p):
        theirs = pin.at[rows_of(p)]
        return remote(theirs, theirs, g_send.at[p], g_recv.at[p], {"panel": p})

    def panels(body):
        each(np_ - 1, lambda index: body(lax.rem(panel + index + 1, np_)))

    panels(lambda p: a_copy(p).start())

    def sum_in():
        panels(lambda p: a_from(p).wait_recv())
        in_recv[panel] = in_send[rows_of(panel), :]
        total = in_recv[0]
        for p in range(1, np_):
            total = total + in_recv[p]
        pin[rows_of(panel), :] = total.astype(BF16)
        panels(lambda p: g_copy(p).start())

    def weigh():
        loads[2].wait()
        inverse = 1.0 / (eig_ref[...] + DAMPING)

        @pl.loop(0, queries // 8)
        def _(q8):
            at = pl.ds(pl.multiple_of(q8 * 8, 8), 8)
            w = qrot[at].astype(F32) * inverse[None]
            w = w.astype(BF16).astype(F32)
            weight[:, at, :] = jnp.swapaxes(w, 0, 1)

        s_send[...] = jnp.zeros_like(s_send)
        proj[...] = jnp.zeros_like(proj)
        for copy in grad_loads:
            copy.wait()

    def valid_in():
        panels(lambda p: g_from(p).wait_recv())
        spots = lax.broadcasted_iota(jnp.int32, (1, length), 1) + tok * length
        for s in range(seqs):
            keep = jnp.where((spots < len_ref[s]) & (mask_ref[s : s + 1, :] == 1), 1.0, 0.0)
            keep = jnp.broadcast_to(keep, (ka, length)).T.astype(BF16)
            at = pl.ds(s * length, length)
            pinv[at, :] = pin[at, :] * keep

    def add_proj(d, part_rows, j):
        at = pl.ds(pl.multiple_of(j * cw, cw), cw)
        proj[d] += lax.dot_general(
            grads[:, :, at].reshape(rows, cw), basis[j, part_rows], NT,
            preferred_element_type=F32,
        )

    def pair_rows(t):
        return pl.ds(pl.multiple_of(t * pair, pair), pair)

    def m_copy(p):
        return remote(
            m_send.at[p], m_recv.at[panel], ms_sem.at[p], mr_sem.at[panel], {"panel": p}
        )

    def m_from(p):
        return remote(m_send.at[p], m_recv.at[p], ms_sem.at[p], mr_sem.at[p], {"panel": p})

    def mix(d, t):
        for s in range(seqs):
            at = pl.ds(s * length, length)
            m = lax.dot_general(
                proj[d, at, :].astype(BF16), pinv[at, :], TN, preferred_element_type=F32
            )
            m_send[pl.ds(t * npc, npc), s] = m.astype(BF16).reshape(npc, kb, ka)
        for j in range(npc):
            p = t * npc + j

            @pl.when(p != panel)
            def _():
                m_copy(p).start()

            @pl.when(p == panel)
            def _():
                m_recv[p] = m_send[p]

    def own_proj():
        own_copy.wait_recv()

        @pl.loop(0, 2 * nc)
        def _(j):
            add_proj(0, pair_rows(tok), j)

    def own_mix():
        valid_in()
        mix(0, tok)

    tasks = {}
    for turn, task in enumerate((weigh, sum_in, own_proj, own_mix)):
        tasks.setdefault(min(turn, nc - 1), []).append(task)

    @pl.loop(0, nc + 2)
    def _(i):
        @pl.when(i < nc)
        def _():
            for d in range(nt - 1):
                pass_copy(d, i, grp, rep, x_send, x_recv, {"tok": from_tok(d)}).wait_recv()
                y_copy(d, i, grp).start()
                cx_copy(d, i, rep).start()

        @pl.when((i > 0) & (i <= nc))
        def _():
            for d in range(nt - 1):
                y_copy(d, i - 1, 1 - grp).wait_recv()
                cy_copy(d, i - 1, rep).start()

        for turn, todo in tasks.items():

            @pl.when(i == turn)
            def _():
                for task in todo:
                    task()

        @pl.when(i > 1)
        def _():
            for d in range(nt - 1):
                t = from_tok(d)
                cx_copy(d, i - 2, 1 - rep).wait_recv()
                add_proj(d + 1, pair_rows(t), grp * nc + i - 2)
                cy_copy(d, i - 2, 1 - rep).wait_recv()
                add_proj(d + 1, pair_rows(t), (1 - grp) * nc + i - 2)

    for d in range(nt - 1):
        mix(d + 1, from_tok(d))

    panels(lambda p: m_from(p).wait_recv())
    total = m_recv[0].astype(F32)
    for p in range(1, np_):
        total = total + m_recv[p].astype(F32)
    m_sum[...] = total

    def step(k8, sums):
        sums = list(sums)
        for j in range(8):
            k = k8 * 8 + j
            w = weight[k]
            for s in range(seqs):
                sums[s] = sums[s] + w * m_sum[s, pl.ds(k, 1), :]
        return tuple(sums)

    sums = lax.fori_loop(
        0, kb // 8, step, tuple(jnp.zeros((queries, ka), F32) for _ in range(seqs))
    )
    ones = jnp.ones((8, ka), F32)
    for s in range(seqs):
        line = lax.dot_general(
            ones, sums[s], NT, precision=lax.Precision.HIGHEST, preferred_element_type=F32
        )
        s_send[s : s + 1, 0:queries] = line[0:1, :]

    me = panel * nt + tok

    def s_copy(index):
        p, t = other(index)
        return remote(
            s_send, s_recv.at[me], ss_sem.at[index], sr_sem.at[me], {"panel": p, "tok": t}
        )

    def s_from(index):
        p, t = other(index)
        who = p * nt + t
        return remote(
            s_send, s_recv.at[who], ss_sem.at[index], sr_sem.at[who], {"panel": p, "tok": t}
        )

    each(np_ * nt - 1, lambda index: s_copy(index).start())
    s_recv[me] = s_send[...]
    each(np_ * nt - 1, lambda index: s_from(index).wait_recv())
    total = s_recv[0]
    for who in range(1, np_ * nt):
        total = total + s_recv[who]
    total_ref[...] = total

    own_copy.wait_send()

    @pl.loop(0, nc)
    def _(i):
        for d in range(nt - 1):
            x_copy(d, i).wait_send()
            y_copy(d, i, grp).wait_send()
            cx_copy(d, i, rep).wait_send()
            cy_copy(d, i, rep).wait_send()
    panels(lambda p: a_copy(p).wait_send())
    panels(lambda p: g_copy(p).wait_send())
    panels(lambda p: m_copy(p).wait_send())
    each(np_ * nt - 1, lambda index: s_copy(index).wait_send())


def finish(total_ref, fail_ref, score_ref, infl_ref):
    seqs, queries = score_ref.shape
    scores = total_ref[:, 0:queries]
    score_ref[...] = scores[0:seqs, :]
    hot = jnp.where(
        lax.broadcasted_iota(jnp.int32, (NFAIL, queries), 0) == fail_ref[...], 1.0, 0.0
    )
    sums = lax.dot_general(
        scores, hot, NT, precision=lax.Precision.HIGHEST, preferred_element_type=F32
    )
    counts = lax.dot_general(
        jnp.ones((8, queries), F32), hot, NT, precision=lax.Precision.HIGHEST,
        preferred_element_type=F32,
    )
    infl_ref[...] = (sums / jnp.maximum(counts, 1.0))[0:seqs, :]


def per_device(
    np_, nt, grads, acts, out_basis, in_basis, eigvals, query_rot, lengths, token_mask, failure_ids
):
    seqs, length, hidden = grads.shape
    rows = seqs * length
    queries, kb, ka = query_rot.shape
    cols = out_basis.shape[1]
    nc = min(2, hidden // 256)
    ngrad = min(8, hidden // 256)
    dma = pltpu.SemaphoreType.DMA
    hop = (nt - 1, nc)
    scratch = [
        pltpu.VMEM(grads.shape, BF16),
        pltpu.VMEM(acts.shape, BF16),
        pltpu.VMEM(in_basis.shape, BF16),
        pltpu.VMEM((2 * nc, cols * nt * 2, hidden // (2 * nc)), BF16),
        pltpu.VMEM(query_rot.shape, BF16),
        pltpu.VMEM((kb, queries, ka), F32),
        pltpu.VMEM((nt, rows, 2 * cols), F32),
        pltpu.VMEM((rows, ka), F32),
        pltpu.VMEM((np_, rows // np_, ka), F32),
        pltpu.VMEM((rows, ka), BF16),
        pltpu.VMEM((rows, ka), BF16),
        pltpu.VMEM((np_, seqs, kb, ka), BF16),
        pltpu.VMEM((np_, seqs, kb, ka), BF16),
        pltpu.VMEM((seqs, kb, ka), F32),
        pltpu.VMEM((8, 128), F32),
        pltpu.VMEM((np_ * nt, 8, 128), F32),
        dma((3,)),
        dma((ngrad,)),
        dma((2 * nc,)),
        dma, dma,
        dma(hop), dma(hop), dma(hop), dma(hop),
        dma(hop), dma(hop), dma(hop), dma(hop),
        dma((np_,)), dma((np_,)), dma((np_,)), dma((np_,)),
        dma((np_,)), dma((np_,)),
        dma((np_ * nt,)), dma((np_ * nt,)),
    ]
    hbm = pl.BlockSpec(memory_space=pl.ANY)
    vmem = pl.BlockSpec(memory_space=pltpu.VMEM)
    total = pl.pallas_call(
        functools.partial(kernel, (np_, nt, nc, ngrad)),
        out_shape=jax.ShapeDtypeStruct((8, 128), F32),
        in_specs=[hbm, hbm, hbm, hbm, vmem, hbm, pl.BlockSpec(memory_space=pltpu.SMEM), vmem],
        out_specs=vmem,
        scratch_shapes=scratch,
        compiler_params=pltpu.CompilerParams(
            collective_id=0, has_side_effects=True, vmem_limit_bytes=56 * 1024 * 1024
        ),
        name="influence",
    )(
        grads, acts, out_basis.T, in_basis, eigvals, query_rot, lengths, token_mask
    )
    scores, influence = pl.pallas_call(
        finish,
        out_shape=(
            jax.ShapeDtypeStruct((seqs, queries), F32),
            jax.ShapeDtypeStruct((seqs, NFAIL), F32),
        ),
        in_specs=[vmem, vmem],
        out_specs=(vmem, vmem),
        name="finish",
    )(total, failure_ids[None, :])
    return scores.T, influence.T


def solution(mesh):
    in_specs = (
        P(("grp", "rep"), "tok", "panel"),
        P(("grp", "rep"), "tok", "panel"),
        P("panel", ("tok", "rep")),
        P("panel", None),
        P("panel", None),
        P("grp", "panel", None),
        P(("grp", "rep")),
        P(("grp", "rep"), "tok"),
        P("grp"),
    )
    out_specs = (P(None, ("grp", "rep")), P(None, ("grp", "rep")))
    return jax.shard_map(
        functools.partial(per_device, mesh.shape["panel"], mesh.shape["tok"]),
        mesh=mesh, in_specs=in_specs, out_specs=out_specs, check_vma=False,
    )
```

```python
import functools

import jax
import jax.numpy as jnp
from jax import lax
from jax.experimental import pallas as pl
from jax.experimental.pallas import tpu as pltpu
from jax.sharding import PartitionSpec as P

NFAIL = 8
DAMPING = 0.1
MESH = pl.DeviceIdType.MESH
F32 = jnp.float32
BF16 = jnp.bfloat16
NT = (((1,), (1,)), ((), ()))
TN = (((0,), (0,)), ((), ()))


def each(count, body):
    if count <= 8:
        for index in range(count):
            body(index)
    else:
        pl.loop(0, count)(body)


def kernel(
    sizes,
    grads_hbm, acts_hbm, basis_hbm, inb_hbm, eig_ref, qrot_hbm, len_ref, mask_ref,
    total_ref,
    grads, acts, inb, basis, qrot, weight, proj, in_send, in_recv, pin, pinv,
    m_send, m_recv, m_sum, s_send, s_recv,
    load_sem, grad_sem, own_sem, own_send, own_recv, x_send, x_recv, y_send, y_recv,
    cx_send, cx_recv, cy_send, cy_recv,
    a_send, a_recv, g_send, g_recv, ms_sem, mr_sem, ss_sem, sr_sem,
):
    np_, nt, nc, ngrad = sizes
    grp, panel = lax.axis_index("grp"), lax.axis_index("panel")
    tok, rep = lax.axis_index("tok"), lax.axis_index("rep")
    seqs, length, hidden = grads.shape
    rows = seqs * length
    queries, kb, ka = qrot.shape
    cols = basis_hbm.shape[0]
    pair = 2 * cols
    npc = pair // kb
    half = hidden // 2
    cw = half // nc
    prow = rows // np_
    gstep = hidden // ngrad

    loads = [
        pltpu.make_async_copy(acts_hbm, acts, load_sem.at[0]),
        pltpu.make_async_copy(inb_hbm, inb, load_sem.at[1]),
        pltpu.make_async_copy(qrot_hbm, qrot, load_sem.at[2]),
    ]
    own_rows = pl.ds(pl.multiple_of((tok * 2 + rep) * cols, cols), cols)
    own_loads = []
    for j in range(2 * nc):
        own_loads.append(
            pltpu.make_async_copy(
                basis_hbm.at[:, pl.ds(j * cw, cw)], basis.at[j, own_rows], own_sem.at[j]
            )
        )
    for copy in own_loads:
        copy.start()
    loads[0].start()
    loads[1].start()

    barrier = pltpu.get_barrier_semaphore()
    pl.semaphore_signal(barrier, inc=1, device_id={"rep": 1 - rep}, device_id_type=MESH)
    pl.semaphore_signal(barrier, inc=1, device_id={"grp": 1 - grp}, device_id_type=MESH)

    def other(index):
        shift = index + 1
        dp, dt = shift // nt, shift % nt
        return lax.rem(panel + dp, np_), lax.rem(tok + dt, nt)

    def greet(index):
        p, t = other(index)
        pl.semaphore_signal(barrier, inc=1, device_id={"panel": p, "tok": t}, device_id_type=MESH)

    each(np_ * nt - 1, greet)
    grad_loads = []
    for g in range(ngrad):
        at = pl.ds(g * gstep, gstep)
        grad_loads.append(
            pltpu.make_async_copy(grads_hbm.at[:, :, at], grads.at[:, :, at], grad_sem.at[g])
        )
    for copy in grad_loads:
        copy.start()
    loads[2].start()
    pl.semaphore_wait(barrier, np_ * nt + 1)

    def block(t, r):
        return pl.ds(pl.multiple_of((t * 2 + r) * cols, cols), cols)

    def remote(src, dst, send, recv, where):
        return pltpu.make_async_remote_copy(
            src_ref=src, dst_ref=dst, send_sem=send, recv_sem=recv,
            device_id=where, device_id_type=MESH,
        )

    def x_copy(d, i):
        mine = basis.at[grp * nc + i, own_rows]
        return remote(
            mine, mine, x_send.at[d, i], x_recv.at[d, i],
            {"tok": lax.rem(tok + d + 1, nt)},
        )

    def from_tok(d):
        return lax.rem(tok + nt - d - 1, nt)

    def pass_copy(d, i, part, r, send, recv, where):
        at = basis.at[part * nc + i, block(from_tok(d), r)]
        return remote(at, at, send.at[d, i], recv.at[d, i], where)

    def y_copy(d, i, part):
        return pass_copy(d, i, part, rep, y_send, y_recv, {"grp": 1 - grp})

    def cx_copy(d, i, r):
        return pass_copy(d, i, grp, r, cx_send, cx_recv, {"rep": 1 - rep})

    def cy_copy(d, i, r):
        return pass_copy(d, i, 1 - grp, r, cy_send, cy_recv, {"rep": 1 - rep})

    own_copy = remote(basis.at[:, own_rows], basis.at[:, own_rows], own_send, own_recv, {"rep": 1 - rep})
    for copy in own_loads:
        copy.wait()

    @pl.loop(0, nc)
    def _(i):
        for d in range(nt - 1):
            x_copy(d, i).start()

    own_copy.start()

    loads[0].wait()
    loads[1].wait()
    in_part = jnp.dot(
        acts[...].reshape(rows, acts.shape[2]), inb[...], preferred_element_type=F32
    )
    in_send[...] = in_part

    def rows_of(p):
        return pl.ds(pl.multiple_of(p * prow, prow), prow)

    def a_copy(p):
        return remote(
            in_send.at[rows_of(p)], in_recv.at[panel], a_send.at[p], a_recv.at[panel],
            {"panel": p},
        )

    def a_from(p):
        return remote(
            in_send.at[rows_of(p)], in_recv.at[p], a_send.at[p], a_recv.at[p], {"panel": p}
        )

    def g_copy(p):
        mine = pin.at[rows_of(panel)]
        return remote(mine, mine, g_send.at[p], g_recv.at[panel], {"panel": p})

    def g_from(p):
        theirs = pin.at[rows_of(p)]
        return remote(theirs, theirs, g_send.at[p], g_recv.at[p], {"panel": p})

    def panels(body):
        each(np_ - 1, lambda index: body(lax.rem(panel + index + 1, np_)))

    panels(lambda p: a_copy(p).start())

    def sum_in():
        panels(lambda p: a_from(p).wait_recv())
        in_recv[panel] = in_send[rows_of(panel), :]
        total = in_recv[0]
        for p in range(1, np_):
            total = total + in_recv[p]
        pin[rows_of(panel), :] = total.astype(BF16)
        panels(lambda p: g_copy(p).start())

    def weigh():
        loads[2].wait()
        inverse = 1.0 / (eig_ref[...] + DAMPING)

        @pl.loop(0, queries // 8)
        def _(q8):
            at = pl.ds(pl.multiple_of(q8 * 8, 8), 8)
            w = qrot[at].astype(F32) * inverse[None]
            w = w.astype(BF16).astype(F32)
            weight[:, at, :] = jnp.swapaxes(w, 0, 1)

        s_send[...] = jnp.zeros_like(s_send)
        proj[...] = jnp.zeros_like(proj)
        for copy in grad_loads:
            copy.wait()

    def valid_in():
        panels(lambda p: g_from(p).wait_recv())
        spots = lax.broadcasted_iota(jnp.int32, (1, length), 1) + tok * length
        for s in range(seqs):
            keep = jnp.where((spots < len_ref[s]) & (mask_ref[s : s + 1, :] == 1), 1.0, 0.0)
            keep = jnp.broadcast_to(keep, (ka, length)).T.astype(BF16)
            at = pl.ds(s * length, length)
            pinv[at, :] = pin[at, :] * keep

    def add_proj(d, part_rows, j):
        at = pl.ds(pl.multiple_of(j * cw, cw), cw)
        proj[d] += lax.dot_general(
            basis[j, part_rows], grads[:, :, at].reshape(rows, cw), NT,
            preferred_element_type=F32,
        )

    def pair_rows(t):
        return pl.ds(pl.multiple_of(t * pair, pair), pair)

    def m_copy(p):
        return remote(
            m_send.at[p], m_recv.at[panel], ms_sem.at[p], mr_sem.at[panel], {"panel": p}
        )

    def m_from(p):
        return remote(m_send.at[p], m_recv.at[p], ms_sem.at[p], mr_sem.at[p], {"panel": p})

    def mix(d, t):
        for s in range(seqs):
            at = pl.ds(s * length, length)
            m = jnp.dot(proj[d, :, at].astype(BF16), pinv[at, :], preferred_element_type=F32)
            m_send[pl.ds(t * npc, npc), s] = m.astype(BF16).reshape(npc, kb, ka)
        for j in range(npc):
            p = t * npc + j

            @pl.when(p != panel)
            def _():
                m_copy(p).start()

            @pl.when(p == panel)
            def _():
                m_recv[p] = m_send[p]

    def own_proj():
        own_copy.wait_recv()

        @pl.loop(0, 2 * nc)
        def _(j):
            add_proj(0, pair_rows(tok), j)

    def own_mix():
        valid_in()
        mix(0, tok)

    tasks = {}
    for turn, task in enumerate((weigh, sum_in, own_proj, own_mix)):
        tasks.setdefault(min(turn, nc - 1), []).append(task)

    @pl.loop(0, nc + 2)
    def _(i):
        @pl.when(i < nc)
        def _():
            for d in range(nt - 1):
                pass_copy(d, i, grp, rep, x_send, x_recv, {"tok": from_tok(d)}).wait_recv()
                y_copy(d, i, grp).start()
                cx_copy(d, i, rep).start()

        @pl.when((i > 0) & (i <= nc))
        def _():
            for d in range(nt - 1):
                y_copy(d, i - 1, 1 - grp).wait_recv()
                cy_copy(d, i - 1, rep).start()

        for turn, todo in tasks.items():

            @pl.when(i == turn)
            def _():
                for task in todo:
                    task()

        @pl.when(i > 1)
        def _():
            for d in range(nt - 1):
                t = from_tok(d)
                cx_copy(d, i - 2, 1 - rep).wait_recv()
                add_proj(d + 1, pair_rows(t), grp * nc + i - 2)
                cy_copy(d, i - 2, 1 - rep).wait_recv()
                add_proj(d + 1, pair_rows(t), (1 - grp) * nc + i - 2)

    for d in range(nt - 1):
        mix(d + 1, from_tok(d))

    panels(lambda p: m_from(p).wait_recv())
    total = m_recv[0].astype(F32)
    for p in range(1, np_):
        total = total + m_recv[p].astype(F32)
    m_sum[...] = total

    def step(k8, sums):
        sums = list(sums)
        for j in range(8):
            k = k8 * 8 + j
            w = weight[k]
            for s in range(seqs):
                sums[s] = sums[s] + w * m_sum[s, pl.ds(k, 1), :]
        return tuple(sums)

    sums = lax.fori_loop(
        0, kb // 8, step, tuple(jnp.zeros((queries, ka), F32) for _ in range(seqs))
    )
    ones = jnp.ones((8, ka), F32)
    for s in range(seqs):
        line = lax.dot_general(
            ones, sums[s], NT, precision=lax.Precision.HIGHEST, preferred_element_type=F32
        )
        s_send[s : s + 1, 0:queries] = line[0:1, :]

    me = panel * nt + tok

    def s_copy(index):
        p, t = other(index)
        return remote(
            s_send, s_recv.at[me], ss_sem.at[index], sr_sem.at[me], {"panel": p, "tok": t}
        )

    def s_from(index):
        p, t = other(index)
        who = p * nt + t
        return remote(
            s_send, s_recv.at[who], ss_sem.at[index], sr_sem.at[who], {"panel": p, "tok": t}
        )

    each(np_ * nt - 1, lambda index: s_copy(index).start())
    s_recv[me] = s_send[...]
    each(np_ * nt - 1, lambda index: s_from(index).wait_recv())
    total = s_recv[0]
    for who in range(1, np_ * nt):
        total = total + s_recv[who]
    total_ref[...] = total

    own_copy.wait_send()

    @pl.loop(0, nc)
    def _(i):
        for d in range(nt - 1):
            x_copy(d, i).wait_send()
            y_copy(d, i, grp).wait_send()
            cx_copy(d, i, rep).wait_send()
            cy_copy(d, i, rep).wait_send()
    panels(lambda p: a_copy(p).wait_send())
    panels(lambda p: g_copy(p).wait_send())
    panels(lambda p: m_copy(p).wait_send())
    each(np_ * nt - 1, lambda index: s_copy(index).wait_send())


def finish(total_ref, fail_ref, score_ref, infl_ref):
    seqs, queries = score_ref.shape
    scores = total_ref[:, 0:queries]
    score_ref[...] = scores[0:seqs, :]
    hot = jnp.where(
        lax.broadcasted_iota(jnp.int32, (NFAIL, queries), 0) == fail_ref[...], 1.0, 0.0
    )
    sums = lax.dot_general(
        scores, hot, NT, precision=lax.Precision.HIGHEST, preferred_element_type=F32
    )
    counts = lax.dot_general(
        jnp.ones((8, queries), F32), hot, NT, precision=lax.Precision.HIGHEST,
        preferred_element_type=F32,
    )
    infl_ref[...] = (sums / jnp.maximum(counts, 1.0))[0:seqs, :]


def per_device(
    np_, nt, grads, acts, out_basis, in_basis, eigvals, query_rot, lengths, token_mask, failure_ids
):
    seqs, length, hidden = grads.shape
    rows = seqs * length
    queries, kb, ka = query_rot.shape
    cols = out_basis.shape[1]
    nc = min(2, hidden // 256)
    ngrad = min(8, hidden // 256)
    dma = pltpu.SemaphoreType.DMA
    hop = (nt - 1, nc)
    scratch = [
        pltpu.VMEM(grads.shape, BF16),
        pltpu.VMEM(acts.shape, BF16),
        pltpu.VMEM(in_basis.shape, BF16),
        pltpu.VMEM((2 * nc, cols * nt * 2, hidden // (2 * nc)), BF16),
        pltpu.VMEM(query_rot.shape, BF16),
        pltpu.VMEM((kb, queries, ka), F32),
        pltpu.VMEM((nt, 2 * cols, rows), F32),
        pltpu.VMEM((rows, ka), F32),
        pltpu.VMEM((np_, rows // np_, ka), F32),
        pltpu.VMEM((rows, ka), BF16),
        pltpu.VMEM((rows, ka), BF16),
        pltpu.VMEM((np_, seqs, kb, ka), BF16),
        pltpu.VMEM((np_, seqs, kb, ka), BF16),
        pltpu.VMEM((seqs, kb, ka), F32),
        pltpu.VMEM((8, 128), F32),
        pltpu.VMEM((np_ * nt, 8, 128), F32),
        dma((3,)),
        dma((ngrad,)),
        dma((2 * nc,)),
        dma, dma,
        dma(hop), dma(hop), dma(hop), dma(hop),
        dma(hop), dma(hop), dma(hop), dma(hop),
        dma((np_,)), dma((np_,)), dma((np_,)), dma((np_,)),
        dma((np_,)), dma((np_,)),
        dma((np_ * nt,)), dma((np_ * nt,)),
    ]
    hbm = pl.BlockSpec(memory_space=pl.ANY)
    vmem = pl.BlockSpec(memory_space=pltpu.VMEM)
    total = pl.pallas_call(
        functools.partial(kernel, (np_, nt, nc, ngrad)),
        out_shape=jax.ShapeDtypeStruct((8, 128), F32),
        in_specs=[hbm, hbm, hbm, hbm, vmem, hbm, pl.BlockSpec(memory_space=pltpu.SMEM), vmem],
        out_specs=vmem,
        scratch_shapes=scratch,
        compiler_params=pltpu.CompilerParams(
            collective_id=0, has_side_effects=True, vmem_limit_bytes=56 * 1024 * 1024
        ),
        name="influence",
    )(
        grads, acts, out_basis.T, in_basis, eigvals, query_rot, lengths, token_mask
    )
    scores, influence = pl.pallas_call(
        finish,
        out_shape=(
            jax.ShapeDtypeStruct((seqs, queries), F32),
            jax.ShapeDtypeStruct((seqs, NFAIL), F32),
        ),
        in_specs=[vmem, vmem],
        out_specs=(vmem, vmem),
        name="finish",
    )(total, failure_ids[None, :])
    return scores.T, influence.T


def solution(mesh):
    in_specs = (
        P(("grp", "rep"), "tok", "panel"),
        P(("grp", "rep"), "tok", "panel"),
        P("panel", ("tok", "rep")),
        P("panel", None),
        P("panel", None),
        P("grp", "panel", None),
        P(("grp", "rep")),
        P(("grp", "rep"), "tok"),
        P("grp"),
    )
    out_specs = (P(None, ("grp", "rep")), P(None, ("grp", "rep")))
    return jax.shard_map(
        functools.partial(per_device, mesh.shape["panel"], mesh.shape["tok"]),
        mesh=mesh, in_specs=in_specs, out_specs=out_specs, check_vma=False,
    )
```
